32 devices in a mesh: ctx: 16 (over z, x, core), head: 2 (over y).
Axes of the slice: x: 2, y: 2, z: 4, core: 2. Of those that a mesh axis runs over, the one named last changes fastest.
Arguments:
- queries: bfloat16 [32768, 4096], P('ctx', 'head'), may hold values from -8 to 8
- key_state_matrix: bfloat16 [32768, 1024], P('ctx', 'head'), may hold values from -4.5 to 4.5
- value_state_matrix: bfloat16 [32768, 1024], P('ctx', 'head'), may hold values from -6 to 6
- selected: int32 [64, 3], P('ctx'), may hold values from -1 to 59, as said below
- out_weight: bfloat16 [4096, 2048], P('head'), may hold values from -0.09375 to 0.09375
Outputs:
- mixed: bfloat16 [32768, 2048], P('ctx', 'head')
The draws below stay inside these ranges and needn't reach their ends.
Inputs may be any that keep to these rules, and one draw needn't show every extreme that they name: `selected`: row j names blocks that lie on lower indices of ctx than block j (the block's index // 4 is the owning index), on three different indices; all rows of one index of ctx name at most one distinct block of each other index; a slot is -1 only when block j's index has fewer than three lower indices, and then exactly the missing slots are -1.
All inputs are finite; a program needn't handle non-finite values.
Results may differ from the reference program's by a relative error of at most 0.015.
Values may be sent and summed in bfloat16 or wider, within the bound.
A program may use at most 192 MiB of HBM per device.

```python
import jax
import jax.numpy as jnp
from jax import lax

QUERY_HEADS = 32
KEY_VALUE_HEADS = 8
HEAD_SIZE = 128
DOUT = 2048
BLOCK_TOKENS = 512
D = 4096
BLK_DEV = 4
SEQUENCE_TOKENS = 32768
BLOCK_COUNT = 64


def draw_queries(key, part):
    key = jax.random.fold_in(key, 1)
    final_output = jnp.clip(jax.random.normal(key, (SEQUENCE_TOKENS, QUERY_HEADS * HEAD_SIZE), jnp.float32), -4.5, 4.5)
    return final_output.astype(jnp.bfloat16)


def draw_key_state_matrix(key, part):
    key = jax.random.fold_in(key, 2)
    final_output = jnp.clip(jax.random.normal(key, (SEQUENCE_TOKENS, KEY_VALUE_HEADS * HEAD_SIZE), jnp.float32), -4.5, 4.5)
    return final_output.astype(jnp.bfloat16)


def draw_selected(key, part):
    key = jax.random.fold_in(key, 3)
    first_key, second_key = jax.random.split(key)
    devices = BLOCK_COUNT // BLK_DEV
    owner = jnp.arange(BLOCK_COUNT) // BLK_DEV
    slots = jnp.arange(devices)
    noise = jax.random.randint(first_key, (BLOCK_COUNT, devices), 0, 1 << 20)
    ranking = noise * devices + slots[None, :]
    forced = (owner[:, None] == devices - 1) & (slots[None, :] == devices - 2)
    ranking = jnp.where(forced, -1, ranking)
    earlier = slots[None, :] < owner[:, None]
    ranking = jnp.where(earlier, ranking, (1 << 30) + slots[None, :])
    picked = jnp.argsort(ranking, axis=1, stable=True)[:, :3]
    within = jax.random.randint(second_key, (devices, devices), 0, BLK_DEV)
    within = within.at[devices - 1, devices - 2].set(BLK_DEV - 1)
    inner = within[owner[:, None], picked]
    final_output = jnp.where(picked < owner[:, None], picked * BLK_DEV + inner, -1)
    return final_output.astype(jnp.int32)


def level_of(key, dims, cuts, low, high):
    level, own = 1.0, jax.random.fold_in(key, 6)
    for dim, shards_of in cuts:
        steps = jnp.exp(jax.random.uniform(jax.random.fold_in(own, dim), (shards_of,), jnp.float32, low / len(cuts), high / len(cuts)))
        level = level * jnp.repeat(steps, dims[dim] // shards_of).reshape([-1 if axis == dim else 1 for axis in range(len(dims))])
    return level


def centred(key, extent, scale, most, pieces=(), held_as=jnp.bfloat16):
    values = jax.random.normal(key, extent, jnp.float32) * scale
    if len(pieces) > 0:
        values = level_of(key, extent, pieces, -0.22, 0.18) * values
    return jnp.clip(values, min=-most, max=most).astype(held_as)


def setup_inputs(seed: int = 0) -> dict:
    seeds = jax.random.split(jax.random.key(seed), 6)
    return {
        "queries": draw_queries(jax.random.fold_in(seeds[5], 71), 0),
        "key_state_matrix": draw_key_state_matrix(jax.random.fold_in(seeds[5], 71), 0),
        "value_state_matrix": centred(seeds[2], (SEQUENCE_TOKENS, KEY_VALUE_HEADS * HEAD_SIZE), 1.0, 6.0, ((0, 16), (1, 2))),
        "selected": draw_selected(jax.random.fold_in(seeds[5], 71), 0),
        "out_weight": centred(seeds[4], (D, DOUT), D ** -0.5, 0.09375, ((0, 2),)),
    }


def reference(queries, key_state_matrix, value_state_matrix, selected, out_weight):
    query_group_size = QUERY_HEADS // KEY_VALUE_HEADS
    score_scale = HEAD_SIZE ** -0.5
    blocked_queries = queries.reshape(BLOCK_COUNT, BLOCK_TOKENS, KEY_VALUE_HEADS, query_group_size, HEAD_SIZE)
    blocked_keys = key_state_matrix.reshape(BLOCK_COUNT, BLOCK_TOKENS, KEY_VALUE_HEADS, HEAD_SIZE)
    blocked_values = value_state_matrix.reshape(BLOCK_COUNT, BLOCK_TOKENS, KEY_VALUE_HEADS, HEAD_SIZE)
    causal = jnp.arange(BLOCK_TOKENS)[:, None] >= jnp.arange(BLOCK_TOKENS)[None, :]

    def one_block(index):
        chosen_row = selected[index]
        picked_block_list = jnp.concatenate([index[None].astype(jnp.int32), jnp.maximum(chosen_row, 0).astype(jnp.int32)])
        gathered_keys = blocked_keys[picked_block_list].reshape(4 * BLOCK_TOKENS, KEY_VALUE_HEADS, HEAD_SIZE).astype(jnp.float32)
        gathered_values = blocked_values[picked_block_list].reshape(4 * BLOCK_TOKENS, KEY_VALUE_HEADS, HEAD_SIZE).astype(jnp.float32)
        live_sel = jnp.broadcast_to(jnp.repeat(chosen_row >= 0, BLOCK_TOKENS)[None, :], (BLOCK_TOKENS, 3 * BLOCK_TOKENS))
        live = jnp.concatenate([causal, live_sel], axis=1)
        query_here = blocked_queries[index].astype(jnp.float32)
        scores = jnp.einsum('qhgd,khd->hgqk', query_here, gathered_keys) * score_scale
        scores = jnp.where(live[None, None], scores, -1e30)
        highest = jnp.max(scores, axis=-1, keepdims=True)
        expon = jnp.exp(scores - highest)
        weights = (expon / jnp.sum(expon, axis=-1, keepdims=True)).astype(jnp.bfloat16)
        output = jnp.einsum('hgqk,khd->qhgd', weights.astype(jnp.float32), gathered_values)
        return output.reshape(BLOCK_TOKENS, QUERY_HEADS * HEAD_SIZE).astype(jnp.bfloat16)

    attended = lax.map(one_block, jnp.arange(BLOCK_COUNT, dtype=jnp.int32)).reshape(SEQUENCE_TOKENS, QUERY_HEADS * HEAD_SIZE)
    return jnp.dot(attended, out_weight, preferred_element_type=jnp.float32).astype(jnp.bfloat16)
```

```python
import functools

import jax
import jax.numpy as jnp
from jax import lax
from jax.experimental import pallas as pl
from jax.experimental.pallas import tpu as pltpu
from jax.sharding import PartitionSpec as P

HEAD_SIZE = 128
BLOCK_TOKENS = 512
ROW_TILE = 256
EXPONENT_SCALE = HEAD_SIZE ** (-0.5) * 1.4426950408889634
NT = (((1,), (1,)), ((), ()))


def pack_kernel(block_ref, key_ref, value_ref, out_ref):
    out_ref[0, :, :HEAD_SIZE] = key_ref[...]
    out_ref[0, :, HEAD_SIZE:] = value_ref[...]


def pack_head(local_block, keys, values, head):
    count = local_block.shape[0]
    spec = pl.BlockSpec((BLOCK_TOKENS, HEAD_SIZE), lambda i, block: (block[i], head))
    return pl.pallas_call(
        pack_kernel,
        grid_spec=pltpu.PrefetchScalarGridSpec(
            num_scalar_prefetch=1,
            grid=(count,),
            in_specs=[spec, spec],
            out_specs=pl.BlockSpec((1, BLOCK_TOKENS, 2 * HEAD_SIZE), lambda i, block: (i, 0, 0)),
        ),
        out_shape=jax.ShapeDtypeStruct((count, BLOCK_TOKENS, 2 * HEAD_SIZE), jnp.bfloat16),
        cost_estimate=pl.CostEstimate(
            flops=0, bytes_accessed=count * BLOCK_TOKENS * 2 * HEAD_SIZE * 4, transcendentals=0
        ),
        name="pack_head",
    )(local_block, keys, values)


def attention_kernel(
    first, group, source_ref, live_ref, query_ref, key_ref, value_ref, far0, far1, far2, out_ref
):
    block = pl.program_id(0) + first
    far = (far0, far1, far2)
    offset = [jnp.where(live_ref[3 * block + j] > 0, 0.0, -1e30).astype(jnp.float32) for j in range(3)]
    ones = jnp.ones((BLOCK_TOKENS, HEAD_SIZE), jnp.bfloat16)
    row = lax.broadcasted_iota(jnp.int32, (ROW_TILE, ROW_TILE), 0)
    column = lax.broadcasted_iota(jnp.int32, (ROW_TILE, ROW_TILE), 1)
    causal = row >= column
    own_value = jnp.concatenate([value_ref[...], ones], axis=1)
    far_value = [jnp.concatenate([ref[0, :, HEAD_SIZE:], ones], axis=1) for ref in far]
    for tile in range(BLOCK_TOKENS // ROW_TILE):
        rows = slice(tile * ROW_TILE, (tile + 1) * ROW_TILE)
        for member in range(group):
            columns = slice(member * HEAD_SIZE, (member + 1) * HEAD_SIZE)
            query = query_ref[rows, columns]
            scores = []
            diagonal = lax.dot_general(
                query, key_ref[rows, :], NT, preferred_element_type=jnp.float32
            )
            diagonal = jnp.where(causal, diagonal, -1e30)
            highest = jnp.max(diagonal, axis=1, keepdims=True)
            scores.append((diagonal, own_value[rows], None))
            if tile > 0:
                before = lax.dot_general(
                    query, key_ref[: tile * ROW_TILE, :], NT, preferred_element_type=jnp.float32
                )
                highest = jnp.maximum(highest, jnp.max(before, axis=1, keepdims=True))
                scores.append((before, own_value[: tile * ROW_TILE], None))
            for j in range(3):
                remote = lax.dot_general(
                    query, far[j][0, :, :HEAD_SIZE], NT, preferred_element_type=jnp.float32
                )
                highest = jnp.maximum(
                    highest, jnp.max(remote, axis=1, keepdims=True) + offset[j]
                )
                scores.append((remote, far_value[j], offset[j]))
            highest = highest * EXPONENT_SCALE
            total = None
            for score, value, shift in scores:
                base = highest if shift is None else highest - shift
                weight = jnp.exp2(score * EXPONENT_SCALE - base).astype(jnp.bfloat16)
                term = jnp.dot(weight, value, preferred_element_type=jnp.float32)
                total = term if total is None else total + term
            out_ref[rows, columns] = (total[:, :HEAD_SIZE] / total[:, HEAD_SIZE:]).astype(
                jnp.bfloat16
            )


def attend_head(source, live, queries, keys, values, arrived, head, group, first, blocks):
    width = group * HEAD_SIZE

    def own(i, source, live):
        return (i + first, head)

    def slot(j):
        return pl.BlockSpec(
            (1, BLOCK_TOKENS, 2 * HEAD_SIZE),
            lambda i, source, live: (source[3 * (i + first) + j], 0, 0),
        )

    pairs = blocks * group * BLOCK_TOKENS * 4 * BLOCK_TOKENS
    return pl.pallas_call(
        functools.partial(attention_kernel, first, group),
        grid_spec=pltpu.PrefetchScalarGridSpec(
            num_scalar_prefetch=2,
            grid=(blocks,),
            in_specs=[
                pl.BlockSpec((BLOCK_TOKENS, width), own),
                pl.BlockSpec((BLOCK_TOKENS, HEAD_SIZE), own),
                pl.BlockSpec((BLOCK_TOKENS, HEAD_SIZE), own),
                slot(0),
                slot(1),
                slot(2),
            ],
            out_specs=pl.BlockSpec((BLOCK_TOKENS, width), lambda i, source, live: (i, 0)),
        ),
        out_shape=jax.ShapeDtypeStruct((blocks * BLOCK_TOKENS, width), jnp.bfloat16),
        compiler_params=pltpu.CompilerParams(vmem_limit_bytes=40 * 1024 * 1024),
        cost_estimate=pl.CostEstimate(
            flops=pairs * HEAD_SIZE * 8,
            bytes_accessed=blocks * BLOCK_TOKENS * 2 * (2 * width + 8 * HEAD_SIZE),
            transcendentals=pairs,
        ),
        name="attend_head",
    )(source, live, queries, keys, values, arrived, arrived, arrived)


def per_device(queries, keys, values, selected, out_weight):
    ctx_count = lax.axis_size("ctx")
    ctx_index = lax.axis_index("ctx")
    head_count = lax.axis_size("head")
    head_index = lax.axis_index("head")
    blk_dev = queries.shape[0] // BLOCK_TOKENS
    kv_heads = keys.shape[1] // HEAD_SIZE
    group = queries.shape[1] // HEAD_SIZE // kv_heads
    width = group * HEAD_SIZE
    out_columns = out_weight.shape[1] // head_count
    request_count = blk_dev * 3

    turns = [[(i, (i + s) % head_count) for i in range(head_count)] for s in range(head_count)]
    weights = []
    for s in range(head_count):
        start = lax.rem(head_index + s, head_count) * out_columns
        share = lax.dynamic_slice_in_dim(out_weight, start, out_columns, axis=1)
        weights.append(share if s == 0 else lax.ppermute(share, "head", turns[s]))

    wanted = selected.reshape(request_count)
    everyone = lax.all_gather(selected, "ctx", axis=0, tiled=True).reshape(ctx_count, request_count)
    asked = jnp.max(jnp.where(everyone // blk_dev == ctx_index, everyone, -1), axis=1)
    local_block = jnp.clip(asked - ctx_index * blk_dev, 0, blk_dev - 1).astype(jnp.int32)
    source = jnp.clip(wanted // blk_dev, 0, ctx_count - 1).astype(jnp.int32)
    live = (wanted >= 0).astype(jnp.int32)

    arrived = []
    for head in range(kv_heads):
        outgoing = pack_head(local_block, keys, values, head)
        arrived.append(
            lax.all_to_all(outgoing, "ctx", split_axis=0, concat_axis=0, tiled=True)
        )

    def project(parts, head):
        total = None
        rows = slice(head * width, (head + 1) * width)
        for part, weight in zip(parts, weights):
            term = jnp.dot(part, weight[rows], preferred_element_type=jnp.float32)
            total = term if total is None else total + term
        return total

    def spread(attended):
        return [attended] + [lax.ppermute(attended, "head", turns[s]) for s in range(1, head_count)]

    total = None
    for head in range(kv_heads - 1):
        attended = attend_head(
            source, live, queries, keys, values, arrived[head], head, group, 0, blk_dev
        )
        term = project(spread(attended), head)
        total = term if total is None else total + term
    head = kv_heads - 1
    half = blk_dev // 2
    outputs = []
    for first, blocks in ((0, half), (half, blk_dev - half)):
        attended = attend_head(
            source, live, queries, keys, values, arrived[head], head, group, first, blocks
        )
        term = project(spread(attended), head)
        rows = slice(first * BLOCK_TOKENS, (first + blocks) * BLOCK_TOKENS)
        outputs.append((term if total is None else total[rows] + term).astype(jnp.bfloat16))
    return jnp.concatenate(outputs, axis=0)


def solution(mesh):
    return jax.shard_map(
        per_device,
        mesh=mesh,
        in_specs=(
            P("ctx", "head"),
            P("ctx", "head"),
            P("ctx", "head"),
            P("ctx", None),
            P("head", None),
        ),
        out_specs=P("ctx", "head"),
        check_vma=False,
    )
```

```python
import functools

import jax
import jax.numpy as jnp
from jax import lax
from jax.experimental import pallas as pl
from jax.experimental.pallas import tpu as pltpu
from jax.sharding import PartitionSpec as P

HEAD_SIZE = 128
BLOCK_TOKENS = 512
ROW_TILE = 256
MATES = 4
EXPONENT_SCALE = HEAD_SIZE ** (-0.5) * 1.4426950408889634
NT = (((1,), (1,)), ((), ()))


def pack_kernel(block_ref, *refs):
    count = len(refs) // 2
    for have, out in zip(refs[:count], refs[count:]):
        out[...] = have[...]


def pack_head(blocks, gathered):
    mates, owners = blocks.shape

    def pick(mate):
        return pl.BlockSpec(
            (1, BLOCK_TOKENS, 2 * HEAD_SIZE),
            lambda i, block: (i, block[mate * owners + i], 0),
        )

    size = owners * BLOCK_TOKENS * 2 * HEAD_SIZE
    return pl.pallas_call(
        pack_kernel,
        grid_spec=pltpu.PrefetchScalarGridSpec(
            num_scalar_prefetch=1,
            grid=(owners,),
            in_specs=[pick(mate) for mate in range(mates)],
            out_specs=[
                pl.BlockSpec((1, BLOCK_TOKENS, 2 * HEAD_SIZE), lambda i, block: (i, 0, 0))
            ]
            * mates,
        ),
        out_shape=[
            jax.ShapeDtypeStruct((owners, BLOCK_TOKENS, 2 * HEAD_SIZE), jnp.bfloat16)
        ]
        * mates,
        cost_estimate=pl.CostEstimate(
            flops=0, bytes_accessed=size * mates * 4, transcendentals=0
        ),
        name="pack_head",
    )(blocks.reshape(-1), *([gathered] * mates))


def attention_kernel(
    first, group, source_ref, live_ref, query_ref, key_ref, value_ref, far0, far1, far2, out_ref
):
    block = pl.program_id(0) + first
    far = (far0, far1, far2)
    offset = [jnp.where(live_ref[3 * block + j] > 0, 0.0, -1e30).astype(jnp.float32) for j in range(3)]
    ones = jnp.ones((BLOCK_TOKENS, HEAD_SIZE), jnp.bfloat16)
    row = lax.broadcasted_iota(jnp.int32, (ROW_TILE, ROW_TILE), 0)
    column = lax.broadcasted_iota(jnp.int32, (ROW_TILE, ROW_TILE), 1)
    causal = row >= column
    own_value = jnp.concatenate([value_ref[...], ones], axis=1)
    far_value = [jnp.concatenate([ref[0, :, HEAD_SIZE:], ones], axis=1) for ref in far]
    for tile in range(BLOCK_TOKENS // ROW_TILE):
        rows = slice(tile * ROW_TILE, (tile + 1) * ROW_TILE)
        for member in range(group):
            columns = slice(member * HEAD_SIZE, (member + 1) * HEAD_SIZE)
            query = query_ref[rows, columns]
            scores = []
            diagonal = lax.dot_general(
                query, key_ref[rows, :], NT, preferred_element_type=jnp.float32
            )
            diagonal = jnp.where(causal, diagonal, -1e30)
            highest = jnp.max(diagonal, axis=1, keepdims=True)
            scores.append((diagonal, own_value[rows], None))
            if tile > 0:
                before = lax.dot_general(
                    query, key_ref[: tile * ROW_TILE, :], NT, preferred_element_type=jnp.float32
                )
                highest = jnp.maximum(highest, jnp.max(before, axis=1, keepdims=True))
                scores.append((before, own_value[: tile * ROW_TILE], None))
            for j in range(3):
                remote = lax.dot_general(
                    query, far[j][0, :, :HEAD_SIZE], NT, preferred_element_type=jnp.float32
                )
                highest = jnp.maximum(
                    highest, jnp.max(remote, axis=1, keepdims=True) + offset[j]
                )
                scores.append((remote, far_value[j], offset[j]))
            highest = highest * EXPONENT_SCALE
            total = None
            for score, value, shift in scores:
                base = highest if shift is None else highest - shift
                weight = jnp.exp2(score * EXPONENT_SCALE - base).astype(jnp.bfloat16)
                term = jnp.dot(weight, value, preferred_element_type=jnp.float32)
                total = term if total is None else total + term
            out_ref[rows, columns] = (total[:, :HEAD_SIZE] / total[:, HEAD_SIZE:]).astype(
                jnp.bfloat16
            )


def attend_head(source, live, queries, keys, values, arrived, head, group, first, blocks):
    width = group * HEAD_SIZE

    def own(i, source, live):
        return (i + first, head)

    def slot(j):
        return pl.BlockSpec(
            (1, BLOCK_TOKENS, 2 * HEAD_SIZE),
            lambda i, source, live: (source[3 * (i + first) + j], 0, 0),
        )

    pairs = blocks * group * BLOCK_TOKENS * 4 * BLOCK_TOKENS
    return pl.pallas_call(
        functools.partial(attention_kernel, first, group),
        grid_spec=pltpu.PrefetchScalarGridSpec(
            num_scalar_prefetch=2,
            grid=(blocks,),
            in_specs=[
                pl.BlockSpec((BLOCK_TOKENS, width), own),
                pl.BlockSpec((BLOCK_TOKENS, HEAD_SIZE), own),
                pl.BlockSpec((BLOCK_TOKENS, HEAD_SIZE), own),
                slot(0),
                slot(1),
                slot(2),
            ],
            out_specs=pl.BlockSpec((BLOCK_TOKENS, width), lambda i, source, live: (i, 0)),
        ),
        out_shape=jax.ShapeDtypeStruct((blocks * BLOCK_TOKENS, width), jnp.bfloat16),
        compiler_params=pltpu.CompilerParams(vmem_limit_bytes=40 * 1024 * 1024),
        cost_estimate=pl.CostEstimate(
            flops=pairs * HEAD_SIZE * 8,
            bytes_accessed=blocks * BLOCK_TOKENS * 2 * (2 * width + 8 * HEAD_SIZE),
            transcendentals=pairs,
        ),
        name="attend_head",
    )(source, live, queries, keys, values, arrived, arrived, arrived)


def per_device(queries, keys, values, selected, out_weight):
    ctx_count = lax.axis_size("ctx")
    ctx_index = lax.axis_index("ctx")
    head_count = lax.axis_size("head")
    head_index = lax.axis_index("head")
    blk_dev = queries.shape[0] // BLOCK_TOKENS
    kv_heads = keys.shape[1] // HEAD_SIZE
    group = queries.shape[1] // HEAD_SIZE // kv_heads
    width = group * HEAD_SIZE
    out_columns = out_weight.shape[1] // head_count
    request_count = blk_dev * 3

    turns = [[(i, (i + s) % head_count) for i in range(head_count)] for s in range(head_count)]
    weights = []
    for s in range(head_count):
        start = lax.rem(head_index + s, head_count) * out_columns
        share = lax.dynamic_slice_in_dim(out_weight, start, out_columns, axis=1)
        weights.append(share if s == 0 else lax.ppermute(share, "head", turns[s]))

    owners = ctx_count // MATES
    columns = [[z * MATES + q for z in range(owners)] for q in range(MATES)]
    gathered = []
    for head in range(kv_heads):
        lanes = slice(head * HEAD_SIZE, (head + 1) * HEAD_SIZE)
        pair = jnp.concatenate([keys[:, lanes], values[:, lanes]], axis=1)
        gathered.append(lax.all_gather(pair, "ctx", axis_index_groups=columns, axis=0))

    wanted = selected.reshape(request_count)
    everyone = lax.all_gather(selected, "ctx", axis=0, tiled=True).reshape(ctx_count, request_count)
    mine = ctx_index % MATES
    mates = jnp.bitwise_xor(ctx_index, jnp.arange(MATES))
    asked = everyone[mates][:, None, :]
    owner_ids = (jnp.arange(owners) * MATES + mine)[None, :, None]
    asked = jnp.max(jnp.where(asked // blk_dev == owner_ids, asked, -1), axis=2)
    blocks = jnp.where(asked >= 0, asked % blk_dev, 0).astype(jnp.int32)
    source = jnp.clip(wanted // blk_dev, 0, ctx_count - 1)
    source = (jnp.bitwise_xor(source % MATES, mine) * owners + source // MATES).astype(jnp.int32)
    live = (wanted >= 0).astype(jnp.int32)
    hops = [[(i, i ^ k) for i in range(ctx_count)] for k in range(MATES)]

    def fetch(head, after):
        have = gathered[head]
        if after is not None:
            have, _ = lax.optimization_barrier((have, after))
        packed = pack_head(blocks, have)
        return [packed[0]] + [lax.ppermute(packed[k], "ctx", hops[k]) for k in range(1, MATES)]

    def project(total, parts, shares, head):
        rows = slice(head * width, (head + 1) * width)
        for part, weight in zip(parts, shares):
            term = jnp.dot(part, weight[rows], preferred_element_type=jnp.float32)
            total = term if total is None else total + term
        return total

    def spread(attended):
        return [attended] + [lax.ppermute(attended, "head", turns[s]) for s in range(1, head_count)]

    last = kv_heads - 1
    fetched = [None] * kv_heads
    fetched[0] = fetch(0, None)
    if last > 0:
        fetched[1] = fetch(1, None)
    total = None
    pending = None
    for head in range(last):
        arrived = jnp.concatenate(fetched[head], axis=0)
        if head == 0:
            arrived, *weights = lax.optimization_barrier((arrived, *weights))
        attended = attend_head(source, live, queries, keys, values, arrived, head, group, 0, blk_dev)
        if head + 2 <= last:
            fetched[head + 2] = fetch(head + 2, attended)
        if pending is not None:
            total = lax.optimization_barrier(project(total, pending, weights, head - 1))
        pending = spread(attended)
    arrived = jnp.concatenate(fetched[last], axis=0)
    if total is not None:
        arrived, total = lax.optimization_barrier((arrived, total))
    half = blk_dev // 2
    parts = []
    for first, count in ((0, half), (half, blk_dev - half)):
        attended = attend_head(
            source, live, queries, keys, values, arrived, last, group, first, count
        )
        parts.append((first, count, spread(attended)))
    if pending is not None:
        total = lax.optimization_barrier(project(total, pending, weights, last - 1))
    outputs = []
    for first, count, part in parts:
        rows = slice(first * BLOCK_TOKENS, (first + count) * BLOCK_TOKENS)
        before = None if total is None else total[rows]
        outputs.append(project(before, part, weights, last).astype(jnp.bfloat16))
    return jnp.concatenate(outputs, axis=0)


def solution(mesh):
    return jax.shard_map(
        per_device,
        mesh=mesh,
        in_specs=(
            P("ctx", "head"),
            P("ctx", "head"),
            P("ctx", "head"),
            P("ctx", None),
            P("head", None),
        ),
        out_specs=P("ctx", "head"),
        check_vma=False,
    )
```

```python
import functools

import jax
import jax.numpy as jnp
from jax import lax
from jax.experimental import pallas as pl
from jax.experimental.pallas import tpu as pltpu
from jax.sharding import PartitionSpec as P

HEAD_SIZE = 128
BLOCK_TOKENS = 512
ROW_TILE = 256
MATES = 4
EXPONENT_SCALE = HEAD_SIZE ** (-0.5) * 1.4426950408889634
NT = (((1,), (1,)), ((), ()))


def pack_kernel(block_ref, *refs):
    count = len(refs) // 2
    for have, out in zip(refs[:count], refs[count:]):
        out[...] = have[...]


def pack_head(blocks, gathered):
    mates, owners = blocks.shape

    def pick(mate):
        return pl.BlockSpec(
            (1, BLOCK_TOKENS, 2 * HEAD_SIZE),
            lambda i, block: (i, block[mate * owners + i], 0),
        )

    size = owners * BLOCK_TOKENS * 2 * HEAD_SIZE
    return pl.pallas_call(
        pack_kernel,
        grid_spec=pltpu.PrefetchScalarGridSpec(
            num_scalar_prefetch=1,
            grid=(owners,),
            in_specs=[pick(mate) for mate in range(mates)],
            out_specs=[
                pl.BlockSpec((1, BLOCK_TOKENS, 2 * HEAD_SIZE), lambda i, block: (i, 0, 0))
            ]
            * mates,
        ),
        out_shape=[
            jax.ShapeDtypeStruct((owners, BLOCK_TOKENS, 2 * HEAD_SIZE), jnp.bfloat16)
        ]
        * mates,
        cost_estimate=pl.CostEstimate(
            flops=0, bytes_accessed=size * mates * 4, transcendentals=0
        ),
        name="pack_head",
    )(blocks.reshape(-1), *([gathered] * mates))


def attention_kernel(
    first, group, source_ref, live_ref, query_ref, key_ref, value_ref, far0, far1, far2, out_ref
):
    block = pl.program_id(0) + first
    far = (far0, far1, far2)
    offset = [jnp.where(live_ref[3 * block + j] > 0, 0.0, -1e30).astype(jnp.float32) for j in range(3)]
    ones = jnp.ones((BLOCK_TOKENS, HEAD_SIZE), jnp.bfloat16)
    row = lax.broadcasted_iota(jnp.int32, (ROW_TILE, ROW_TILE), 0)
    column = lax.broadcasted_iota(jnp.int32, (ROW_TILE, ROW_TILE), 1)
    causal = row >= column
    own_value = jnp.concatenate([value_ref[...], ones], axis=1)
    far_value = [jnp.concatenate([ref[0, :, HEAD_SIZE:], ones], axis=1) for ref in far]
    for tile in range(BLOCK_TOKENS // ROW_TILE):
        rows = slice(tile * ROW_TILE, (tile + 1) * ROW_TILE)
        for member in range(group):
            columns = slice(member * HEAD_SIZE, (member + 1) * HEAD_SIZE)
            query = query_ref[rows, columns]
            scores = []
            diagonal = lax.dot_general(
                query, key_ref[rows, :], NT, preferred_element_type=jnp.float32
            )
            diagonal = jnp.where(causal, diagonal, -1e30)
            highest = jnp.max(diagonal, axis=1, keepdims=True)
            scores.append((diagonal, own_value[rows], None))
            if tile > 0:
                before = lax.dot_general(
                    query, key_ref[: tile * ROW_TILE, :], NT, preferred_element_type=jnp.float32
                )
                highest = jnp.maximum(highest, jnp.max(before, axis=1, keepdims=True))
                scores.append((before, own_value[: tile * ROW_TILE], None))
            for j in range(3):
                remote = lax.dot_general(
                    query, far[j][0, :, :HEAD_SIZE], NT, preferred_element_type=jnp.float32
                )
                highest = jnp.maximum(
                    highest, jnp.max(remote, axis=1, keepdims=True) + offset[j]
                )
                scores.append((remote, far_value[j], offset[j]))
            highest = highest * EXPONENT_SCALE
            total = None
            for score, value, shift in scores:
                base = highest if shift is None else highest - shift
                weight = jnp.exp2(score * EXPONENT_SCALE - base).astype(jnp.bfloat16)
                term = jnp.dot(weight, value, preferred_element_type=jnp.float32)
                total = term if total is None else total + term
            out_ref[rows, columns] = (total[:, :HEAD_SIZE] / total[:, HEAD_SIZE:]).astype(
                jnp.bfloat16
            )


def attend_head(source, live, queries, keys, values, arrived, head, group, first, blocks):
    width = group * HEAD_SIZE

    def own(i, source, live):
        return (i + first, head)

    def slot(j):
        return pl.BlockSpec(
            (1, BLOCK_TOKENS, 2 * HEAD_SIZE),
            lambda i, source, live: (source[3 * (i + first) + j], 0, 0),
        )

    pairs = blocks * group * BLOCK_TOKENS * 4 * BLOCK_TOKENS
    return pl.pallas_call(
        functools.partial(attention_kernel, first, group),
        grid_spec=pltpu.PrefetchScalarGridSpec(
            num_scalar_prefetch=2,
            grid=(blocks,),
            in_specs=[
                pl.BlockSpec((BLOCK_TOKENS, width), own),
                pl.BlockSpec((BLOCK_TOKENS, HEAD_SIZE), own),
                pl.BlockSpec((BLOCK_TOKENS, HEAD_SIZE), own),
                slot(0),
                slot(1),
                slot(2),
            ],
            out_specs=pl.BlockSpec((BLOCK_TOKENS, width), lambda i, source, live: (i, 0)),
        ),
        out_shape=jax.ShapeDtypeStruct((blocks * BLOCK_TOKENS, width), jnp.bfloat16),
        compiler_params=pltpu.CompilerParams(vmem_limit_bytes=40 * 1024 * 1024),
        cost_estimate=pl.CostEstimate(
            flops=pairs * HEAD_SIZE * 8,
            bytes_accessed=blocks * BLOCK_TOKENS * 2 * (2 * width + 8 * HEAD_SIZE),
            transcendentals=pairs,
        ),
        name="attend_head",
    )(source, live, queries, keys, values, arrived, arrived, arrived)


def per_device(queries, keys, values, selected, out_weight):
    ctx_count = lax.axis_size("ctx")
    ctx_index = lax.axis_index("ctx")
    head_count = lax.axis_size("head")
    head_index = lax.axis_index("head")
    blk_dev = queries.shape[0] // BLOCK_TOKENS
    kv_heads = keys.shape[1] // HEAD_SIZE
    group = queries.shape[1] // HEAD_SIZE // kv_heads
    width = group * HEAD_SIZE
    out_columns = out_weight.shape[1] // head_count
    request_count = blk_dev * 3

    turns = [[(i, (i + s) % head_count) for i in range(head_count)] for s in range(head_count)]
    weights = []
    for s in range(head_count):
        start = lax.rem(head_index + s, head_count) * out_columns
        share = lax.dynamic_slice_in_dim(out_weight, start, out_columns, axis=1)
        weights.append(share if s == 0 else lax.ppermute(share, "head", turns[s]))

    owners = ctx_count // MATES
    columns = [[z * MATES + q for z in range(owners)] for q in range(MATES)]
    chained = kv_heads - 1 if kv_heads > 2 else None
    gathered = [None] * kv_heads
    for head in range(kv_heads):
        lanes = slice(head * HEAD_SIZE, (head + 1) * HEAD_SIZE)
        pair = jnp.concatenate([keys[:, lanes], values[:, lanes]], axis=1)
        if head == chained:
            chain = [pair]
            for s in range(1, owners):
                up = [(i, i + MATES) for i in range((s - 1) * MATES, ctx_count - MATES)]
                chain.append(lax.ppermute(chain[-1], "ctx", up))
        else:
            gathered[head] = lax.all_gather(pair, "ctx", axis_index_groups=columns, axis=0)
    if chained is not None:
        gathered[0], *chain = lax.optimization_barrier((gathered[0], *chain))
        gathered[chained] = jnp.stack(chain, axis=0)

    wanted = selected.reshape(request_count)
    everyone = lax.all_gather(selected, "ctx", axis=0, tiled=True).reshape(ctx_count, request_count)
    mine = ctx_index % MATES
    mates = jnp.bitwise_xor(ctx_index, jnp.arange(MATES))
    asked = everyone[mates][:, None, :]
    owner_ids = (jnp.arange(owners) * MATES + mine)[None, :, None]
    asked = jnp.max(jnp.where(asked // blk_dev == owner_ids, asked, -1), axis=2)
    blocks = jnp.where(asked >= 0, asked % blk_dev, 0).astype(jnp.int32)
    place = ctx_index // MATES
    upward = lax.rem(place - jnp.arange(owners) + owners, owners)
    chain_blocks = blocks[:, upward]
    wanted_owner = jnp.clip(wanted // blk_dev, 0, ctx_count - 1)
    sender = jnp.bitwise_xor(wanted_owner % MATES, mine) * owners
    source = (sender + wanted_owner // MATES).astype(jnp.int32)
    distance = lax.rem(place - wanted_owner // MATES + owners, owners)
    chain_source = (sender + distance).astype(jnp.int32)
    live = (wanted >= 0).astype(jnp.int32)
    hops = [[(i, i ^ k) for i in range(ctx_count)] for k in range(MATES)]

    def fetch(head, after):
        have = gathered[head]
        if after is not None:
            have, _ = lax.optimization_barrier((have, after))
        packed = pack_head(chain_blocks if head == chained else blocks, have)
        return [packed[0]] + [lax.ppermute(packed[k], "ctx", hops[k]) for k in range(1, MATES)]

    def project(total, parts, shares, head):
        rows = slice(head * width, (head + 1) * width)
        for part, weight in zip(parts, shares):
            term = jnp.dot(part, weight[rows], preferred_element_type=jnp.float32)
            total = term if total is None else total + term
        return total

    def spread(attended):
        return [attended] + [lax.ppermute(attended, "head", turns[s]) for s in range(1, head_count)]

    def attend(head, arrived, first, count):
        places = chain_source if head == chained else source
        return attend_head(places, live, queries, keys, values, arrived, head, group, first, count)

    order = list(range(kv_heads))
    if chained is not None:
        order = [0, chained] + list(range(1, chained))
    last = order[-1]
    fetched = {order[0]: fetch(order[0], None)}
    if chained is not None:
        fetched[chained] = fetch(chained, None)
    total = None
    pending = []
    previous = None
    for head in order[:-1]:
        if head not in fetched:
            fetched[head] = fetch(head, previous)
        arrived = jnp.concatenate(fetched[head], axis=0)
        if previous is None:
            arrived, *weights = lax.optimization_barrier((arrived, *weights))
        elif len(pending) > 1:
            total = project(total, pending[0][1], weights, pending[0][0])
            pending = pending[1:]
            arrived, total = lax.optimization_barrier((arrived, total))
        previous = attend(head, arrived, 0, blk_dev)
        pending.append((head, spread(previous)))
    if last not in fetched:
        fetched[last] = fetch(last, previous)
    arrived = jnp.concatenate(fetched[last], axis=0)
    for head, part in pending:
        total = project(total, part, weights, head)
        arrived, total = lax.optimization_barrier((arrived, total))
    half = blk_dev // 2
    parts = []
    for first, count in ((0, half), (half, blk_dev - half)):
        parts.append((first, count, spread(attend(last, arrived, first, count))))
    outputs = []
    for first, count, part in parts:
        rows = slice(first * BLOCK_TOKENS, (first + count) * BLOCK_TOKENS)
        before = None if total is None else total[rows]
        outputs.append(project(before, part, weights, last).astype(jnp.bfloat16))
    return jnp.concatenate(outputs, axis=0)


def solution(mesh):
    return jax.shard_map(
        per_device,
        mesh=mesh,
        in_specs=(
            P("ctx", "head"),
            P("ctx", "head"),
            P("ctx", "head"),
            P("ctx", None),
            P("head", None),
        ),
        out_specs=P("ctx", "head"),
        check_vma=False,
    )
```

```python
import functools

import jax
import jax.numpy as jnp
from jax import lax
from jax.experimental import pallas as pl
from jax.experimental.pallas import tpu as pltpu
from jax.sharding import PartitionSpec as P

HEAD_SIZE = 128
BLOCK_TOKENS = 512
ROW_TILE = 256
MATES = 4
EXPONENT_SCALE = HEAD_SIZE ** (-0.5) * 1.4426950408889634
NT = (((1,), (1,)), ((), ()))


def pack_kernel(block_ref, *refs):
    count = len(refs) // 2
    for have, out in zip(refs[:count], refs[count:]):
        out[...] = have[...]


def pack_head(blocks, gathered):
    mates, owners = blocks.shape

    def pick(mate):
        return pl.BlockSpec(
            (1, BLOCK_TOKENS, 2 * HEAD_SIZE),
            lambda i, block: (i, block[mate * owners + i], 0),
        )

    size = owners * BLOCK_TOKENS * 2 * HEAD_SIZE
    return pl.pallas_call(
        pack_kernel,
        grid_spec=pltpu.PrefetchScalarGridSpec(
            num_scalar_prefetch=1,
            grid=(owners,),
            in_specs=[pick(mate) for mate in range(mates)],
            out_specs=[
                pl.BlockSpec((1, BLOCK_TOKENS, 2 * HEAD_SIZE), lambda i, block: (i, 0, 0))
            ]
            * mates,
        ),
        out_shape=[
            jax.ShapeDtypeStruct((owners, BLOCK_TOKENS, 2 * HEAD_SIZE), jnp.bfloat16)
        ]
        * mates,
        cost_estimate=pl.CostEstimate(
            flops=0, bytes_accessed=size * mates * 4, transcendentals=0
        ),
        name="pack_head",
    )(blocks.reshape(-1), *([gathered] * mates))


def attention_kernel(
    first, group, source_ref, live_ref, query_ref, key_ref, value_ref, far0, far1, far2, out_ref
):
    block = pl.program_id(0) + first
    far = (far0, far1, far2)
    offset = [jnp.where(live_ref[3 * block + j] > 0, 0.0, -1e30).astype(jnp.float32) for j in range(3)]
    ones = jnp.ones((BLOCK_TOKENS, HEAD_SIZE), jnp.bfloat16)
    row = lax.broadcasted_iota(jnp.int32, (ROW_TILE, ROW_TILE), 0)
    column = lax.broadcasted_iota(jnp.int32, (ROW_TILE, ROW_TILE), 1)
    causal = row >= column
    own_value = jnp.concatenate([value_ref[...], ones], axis=1)
    far_value = [jnp.concatenate([ref[0, :, HEAD_SIZE:], ones], axis=1) for ref in far]
    for tile in range(BLOCK_TOKENS // ROW_TILE):
        rows = slice(tile * ROW_TILE, (tile + 1) * ROW_TILE)
        for member in range(group):
            columns = slice(member * HEAD_SIZE, (member + 1) * HEAD_SIZE)
            query = query_ref[rows, columns]
            scores = []
            diagonal = lax.dot_general(
                query, key_ref[rows, :], NT, preferred_element_type=jnp.float32
            )
            diagonal = jnp.where(causal, diagonal, -1e30)
            highest = jnp.max(diagonal, axis=1, keepdims=True)
            scores.append((diagonal, own_value[rows], None))
            if tile > 0:
                before = lax.dot_general(
                    query, key_ref[: tile * ROW_TILE, :], NT, preferred_element_type=jnp.float32
                )
                highest = jnp.maximum(highest, jnp.max(before, axis=1, keepdims=True))
                scores.append((before, own_value[: tile * ROW_TILE], None))
            for j in range(3):
                remote = lax.dot_general(
                    query, far[j][0, :, :HEAD_SIZE], NT, preferred_element_type=jnp.float32
                )
                highest = jnp.maximum(
                    highest, jnp.max(remote, axis=1, keepdims=True) + offset[j]
                )
                scores.append((remote, far_value[j], offset[j]))
            highest = highest * EXPONENT_SCALE
            total = None
            for score, value, shift in scores:
                base = highest if shift is None else highest - shift
                weight = jnp.exp2(score * EXPONENT_SCALE - base).astype(jnp.bfloat16)
                term = jnp.dot(weight, value, preferred_element_type=jnp.float32)
                total = term if total is None else total + term
            out_ref[rows, columns] = (total[:, :HEAD_SIZE] / total[:, HEAD_SIZE:]).astype(
                jnp.bfloat16
            )


def attend_head(source, live, queries, keys, values, arrived, head, group, first, blocks):
    width = group * HEAD_SIZE

    def own(i, source, live):
        return (i + first, head)

    def slot(j):
        return pl.BlockSpec(
            (1, BLOCK_TOKENS, 2 * HEAD_SIZE),
            lambda i, source, live: (source[3 * (i + first) + j], 0, 0),
        )

    pairs = blocks * group * BLOCK_TOKENS * 4 * BLOCK_TOKENS
    return pl.pallas_call(
        functools.partial(attention_kernel, first, group),
        grid_spec=pltpu.PrefetchScalarGridSpec(
            num_scalar_prefetch=2,
            grid=(blocks,),
            in_specs=[
                pl.BlockSpec((BLOCK_TOKENS, width), own),
                pl.BlockSpec((BLOCK_TOKENS, HEAD_SIZE), own),
                pl.BlockSpec((BLOCK_TOKENS, HEAD_SIZE), own),
                slot(0),
                slot(1),
                slot(2),
            ],
            out_specs=pl.BlockSpec((BLOCK_TOKENS, width), lambda i, source, live: (i, 0)),
        ),
        out_shape=jax.ShapeDtypeStruct((blocks * BLOCK_TOKENS, width), jnp.bfloat16),
        compiler_params=pltpu.CompilerParams(vmem_limit_bytes=40 * 1024 * 1024),
        cost_estimate=pl.CostEstimate(
            flops=pairs * HEAD_SIZE * 8,
            bytes_accessed=blocks * BLOCK_TOKENS * 2 * (2 * width + 8 * HEAD_SIZE),
            transcendentals=pairs,
        ),
        name="attend_head",
    )(source, live, queries, keys, values, arrived, arrived, arrived)


def per_device(queries, keys, values, selected, out_weight):
    ctx_count = lax.axis_size("ctx")
    ctx_index = lax.axis_index("ctx")
    head_count = lax.axis_size("head")
    head_index = lax.axis_index("head")
    blk_dev = queries.shape[0] // BLOCK_TOKENS
    kv_heads = keys.shape[1] // HEAD_SIZE
    group = queries.shape[1] // HEAD_SIZE // kv_heads
    width = group * HEAD_SIZE
    out_columns = out_weight.shape[1] // head_count
    request_count = blk_dev * 3

    turns = [[(i, (i + s) % head_count) for i in range(head_count)] for s in range(head_count)]
    weights = []
    for s in range(head_count):
        start = lax.rem(head_index + s, head_count) * out_columns
        share = lax.dynamic_slice_in_dim(out_weight, start, out_columns, axis=1)
        weights.append(share if s == 0 else lax.ppermute(share, "head", turns[s]))

    everyone = lax.all_gather(selected, "ctx", axis=0, tiled=True).reshape(ctx_count, request_count)
    owners = ctx_count // MATES
    columns = [[z * MATES + q for z in range(owners)] for q in range(MATES)]
    chained = kv_heads - 1 if kv_heads > 2 else None
    gathered = [None] * kv_heads
    for head in range(kv_heads):
        lanes = slice(head * HEAD_SIZE, (head + 1) * HEAD_SIZE)
        pair = jnp.concatenate([keys[:, lanes], values[:, lanes]], axis=1)
        if head == chained:
            pair, everyone = lax.optimization_barrier((pair, everyone))
            chain = [pair]
            for s in range(1, owners):
                up = [(i, i + MATES) for i in range((s - 1) * MATES, ctx_count - MATES)]
                chain.append(lax.ppermute(chain[-1], "ctx", up))
        else:
            gathered[head] = lax.all_gather(pair, "ctx", axis_index_groups=columns, axis=0)
    if chained is not None:
        gathered[0], *chain[:-1] = lax.optimization_barrier((gathered[0], *chain[:-1]))
        gathered[chained] = jnp.stack(chain, axis=0)

    wanted = selected.reshape(request_count)
    mine = ctx_index % MATES
    mates = jnp.bitwise_xor(ctx_index, jnp.arange(MATES))
    asked = everyone[mates][:, None, :]
    owner_ids = (jnp.arange(owners) * MATES + mine)[None, :, None]
    asked = jnp.max(jnp.where(asked // blk_dev == owner_ids, asked, -1), axis=2)
    blocks = jnp.where(asked >= 0, asked % blk_dev, 0).astype(jnp.int32)
    place = ctx_index // MATES
    upward = lax.rem(place - jnp.arange(owners) + owners, owners)
    chain_blocks = blocks[:, upward]
    wanted_owner = jnp.clip(wanted // blk_dev, 0, ctx_count - 1)
    sender = jnp.bitwise_xor(wanted_owner % MATES, mine) * owners
    source = (sender + wanted_owner // MATES).astype(jnp.int32)
    distance = lax.rem(place - wanted_owner // MATES + owners, owners)
    chain_source = (sender + distance).astype(jnp.int32)
    live = (wanted >= 0).astype(jnp.int32)
    hops = [[(i, i ^ k) for i in range(ctx_count)] for k in range(MATES)]

    def fetch(head, after):
        have = gathered[head]
        if after is not None:
            have, _ = lax.optimization_barrier((have, after))
        packed = pack_head(chain_blocks if head == chained else blocks, have)
        return [packed[0]] + [lax.ppermute(packed[k], "ctx", hops[k]) for k in range(1, MATES)]

    def project(total, parts, shares, head):
        rows = slice(head * width, (head + 1) * width)
        for part, weight in zip(parts, shares):
            term = jnp.dot(part, weight[rows], preferred_element_type=jnp.float32)
            total = term if total is None else total + term
        return total

    def spread(attended):
        return [attended] + [lax.ppermute(attended, "head", turns[s]) for s in range(1, head_count)]

    def attend(head, arrived, first, count):
        places = chain_source if head == chained else source
        return attend_head(places, live, queries, keys, values, arrived, head, group, first, count)

    order = list(range(kv_heads))
    if chained is not None:
        order = [0, chained] + list(range(1, chained))
    last = order[-1]
    fetched = {order[0]: fetch(order[0], None)}
    total = None
    pending = []
    done = []
    for step, head in enumerate(order[:-1]):
        parts = fetched[head]
        if head == chained:
            following = order[step + 1]
            fetched[following] = fetch(following, done[0])
            parts[0], fetched[following][0] = lax.optimization_barrier(
                (parts[0], fetched[following][0])
            )
        arrived = jnp.concatenate(parts, axis=0)
        if not done:
            arrived, *weights = lax.optimization_barrier((arrived, *weights))
        elif len(pending) > 1:
            total = project(total, pending[0][1], weights, pending[0][0])
            pending = pending[1:]
            arrived, total = lax.optimization_barrier((arrived, total))
        done.append(attend(head, arrived, 0, blk_dev))
        following = order[step + 1]
        if following not in fetched:
            fetched[following] = fetch(following, done[-1])
        pending.append((head, spread(done[-1])))
    arrived = jnp.concatenate(fetched[last], axis=0)
    for head, part in pending:
        total = project(total, part, weights, head)
        arrived, total = lax.optimization_barrier((arrived, total))
    half = blk_dev // 2
    parts = []
    for first, count in ((0, half), (half, blk_dev - half)):
        parts.append((first, count, spread(attend(last, arrived, first, count))))
    outputs = []
    for first, count, part in parts:
        rows = slice(first * BLOCK_TOKENS, (first + count) * BLOCK_TOKENS)
        before = None if total is None else total[rows]
        outputs.append(project(before, part, weights, last).astype(jnp.bfloat16))
    return jnp.concatenate(outputs, axis=0)


def solution(mesh):
    return jax.shard_map(
        per_device,
        mesh=mesh,
        in_specs=(
            P("ctx", "head"),
            P("ctx", "head"),
            P("ctx", "head"),
            P("ctx", None),
            P("head", None),
        ),
        out_specs=P("ctx", "head"),
        check_vma=False,
    )
```
